32 devices in a mesh: ctx: 4 (over z), tp: 4 (over y, core), dp: 2 (over x).
Axes of the slice: x: 2, y: 2, z: 4, core: 2. Of those that a mesh axis runs over, the one named last changes fastest.
Arguments:
- queries: bfloat16 [4096, 2048], P(('dp', 'ctx'), 'tp'), parts along dimension 0, may hold values from -6 to 6
- keys: bfloat16 [4096, 512], P(('dp', 'ctx'), 'tp'), parts along dimension 0, may hold values from -6 to 6
- values: bfloat16 [4096, 512], P(('dp', 'ctx'), 'tp'), parts along dimension 0, may hold values from -6 to 6
- outputs: bfloat16 [4096, 2048], P(('dp', 'ctx'), 'tp'), parts along dimension 0, may hold values from -4 to 4
- out_grads: bfloat16 [4096, 2048], P(('dp', 'ctx'), 'tp'), parts along dimension 0, may hold values from -6 to 6
- log_norms: float32 [16, 4096], P('tp', ('dp', 'ctx')), parts along dimension 1, may hold values from 3 to 6
- stretch_order: int32 [16], P('dp'), parts along dimension 0, may hold values from 0 to 7, each once
Outputs:
- grad_queries: bfloat16 [4096, 2048], P(('dp', 'ctx'), 'tp'), parts along dimension 0
- grad_keys: bfloat16 [4096, 512], P(('dp', 'ctx'), 'tp'), parts along dimension 0
- grad_values: bfloat16 [4096, 512], P(('dp', 'ctx'), 'tp'), parts along dimension 0
The draws below stay inside these ranges and needn't reach their ends.
There are 2 independent parts, one for each index of `dp`. The reference program is written for one: setup_inputs(seed, part) draws one part's arguments, and reference() takes and returns one part's arrays. A program takes and returns all parts, laid end to end along the dimension named above; each array names one. Nothing has to cross between parts.
Inputs may be any that keep to these rules, and one draw needn't show every extreme that they name: stretch_order is a permutation of the 8 sequence blocks of 256 tokens.
All inputs are finite; a program needn't handle non-finite values.
Results may differ from the reference program's by a relative error of at most 0.023.
Values may be sent and summed in bfloat16 or wider, within the bound.
No kernel may reach another device: no remote copies, remote signals or barrier semaphores. Data moves between devices by JAX's collectives and lax.ppermute only.
A program may use at most 64 MiB of HBM per device.

```python
import jax
import jax.numpy as jnp
from jax import lax

QH = 16
KVH = 4
HD = 128
STRETCH = 256
SEQ = 2048
N_CTX = 4


def block_levels(stream_key, extent, shards, low, top_value):
    def one(axis_at, shards_of):
        draws = jax.random.uniform(jax.random.fold_in(jax.random.fold_in(stream_key, 6), axis_at), (shards_of,), jnp.float32, low / len(shards), top_value / len(shards))
        return jnp.repeat(jnp.exp(draws), extent[axis_at] // shards_of).reshape((-1,) + (1,) * (len(extent) - axis_at - 1))

    factor_of = one(*shards[0])
    for cut in shards[1:]:
        factor_of = factor_of * one(*cut)
    return factor_of


def centred(stream_key, extent, spread, reach, shards=(), kind=jnp.bfloat16):
    drawn = spread * jax.random.normal(stream_key, extent, jnp.float32)
    if shards:
        drawn = drawn * block_levels(stream_key, extent, shards, -0.22, 0.18)
    return jnp.clip(drawn, -reach, reach).astype(kind)


def setup_inputs(seed: int = 0, part: int = 0) -> dict:
    key_of = jax.random.split(jax.random.key(seed), 8)
    part_keys = jax.random.split(jax.random.fold_in(key_of[7], part), 8)
    return {
        "queries": centred(part_keys[0], (SEQ, QH * HD), 1.0, 6.0, ((0, 4), (1, 4))),
        "keys": centred(part_keys[1], (SEQ, KVH * HD), 1.0, 6.0, ((0, 4), (1, 4))),
        "values": centred(part_keys[2], (SEQ, KVH * HD), 1.0, 6.0, ((0, 4), (1, 4))),
        "outputs": centred(part_keys[3], (SEQ, QH * HD), 0.3, 4.0, ((0, 4), (1, 4))),
        "out_grads": centred(part_keys[4], (SEQ, QH * HD), 1.0, 6.0, ((0, 4), (1, 4))),
        "log_norms": jnp.clip(3.0 + 3.0 * jax.random.uniform(part_keys[5], (QH, SEQ), jnp.float32) ** block_levels(part_keys[5], (QH, SEQ), ((0, 4), (1, 4)), -0.2, 0.2), 3.0, 6.0),
        "stretch_order": jax.random.permutation(part_keys[6], 2 * N_CTX).astype(jnp.int32),
    }


def reference(queries, keys, values, outputs, out_grads, log_norms, stretch_order):
    seq_len = queries.shape[0]
    group_size = QH // KVH
    score_scale = HD ** -0.5
    row_index = jnp.arange(seq_len, dtype=jnp.int32)
    position = jnp.take(stretch_order, row_index // STRETCH) * STRETCH + row_index % STRETCH
    allowed = position[None, :] <= position[:, None]
    query_heads = queries.reshape(seq_len, KVH, group_size, HD).transpose(1, 2, 0, 3)
    grad_heads = out_grads.reshape(seq_len, KVH, group_size, HD).transpose(1, 2, 0, 3)
    output_heads = outputs.reshape(seq_len, KVH, group_size, HD).transpose(1, 2, 0, 3)
    key_heads = keys.reshape(seq_len, KVH, HD).transpose(1, 0, 2)
    value_heads = values.reshape(seq_len, KVH, HD).transpose(1, 0, 2)
    norm_heads = log_norms.reshape(KVH, group_size, seq_len)

    def one_head(operands):
        query_one, grad_one, output_one, key_one, value_one, norm_one = operands
        query_f = query_one.astype(jnp.float32)
        grad_f = grad_one.astype(jnp.float32)
        key_f = key_one.astype(jnp.float32)
        value_f = value_one.astype(jnp.float32)
        delta_rows = jnp.sum(grad_f * output_one.astype(jnp.float32), axis=-1)
        scores = jnp.einsum("gqd,kd->gqk", query_f, key_f) * score_scale
        probs = jnp.where(allowed[None], jnp.exp(scores - norm_one[:, :, None]), jnp.float32(0.0))
        probs_low = probs.astype(jnp.bfloat16).astype(jnp.float32)
        grad_value = jnp.einsum("gqk,gqd->kd", probs_low, grad_f)
        grad_probs = jnp.einsum("gqd,kd->gqk", grad_f, value_f)
        grad_scores = (score_scale * probs * (grad_probs - delta_rows[:, :, None])).astype(jnp.bfloat16).astype(jnp.float32)
        grad_query = jnp.einsum("gqk,kd->gqd", grad_scores, key_f)
        grad_key = jnp.einsum("gqk,gqd->kd", grad_scores, query_f)
        return grad_query, grad_key, grad_value

    grad_query, grad_key, grad_value = lax.map(one_head, (query_heads, grad_heads, output_heads, key_heads, value_heads, norm_heads))
    grad_queries = grad_query.transpose(2, 0, 1, 3).reshape(seq_len, QH * HD).astype(jnp.bfloat16)
    grad_keys = grad_key.transpose(1, 0, 2).reshape(seq_len, KVH * HD).astype(jnp.bfloat16)
    grad_values = grad_value.transpose(1, 0, 2).reshape(seq_len, KVH * HD).astype(jnp.bfloat16)
    return (grad_queries, grad_keys, grad_values)
```

```python
import functools
import math

import jax
import jax.numpy as jnp
from jax import lax
from jax.experimental import pallas as pl
from jax.experimental.pallas import tpu as pltpu
from jax.sharding import PartitionSpec as P

HD = 128
SCALE = HD ** (-0.5)
LOG2E = math.log2(math.e)
F32 = jnp.float32
BF16 = jnp.bfloat16
VMEM_LIMIT = 48 * 1024 * 1024


def tile_terms(a, b, diagonal, key, value, key_t, qt, q, gt, g, norm, delta, dqt, dk, dv):
    size = key.shape[0]
    heads = norm.shape[0]
    for h in range(heads):
        cols = pl.ds(h * size, size)
        rows = pl.ds(a * size, size)
        lanes = pl.ds(h * HD, HD)
        scores = jnp.dot(key, qt[a, :, cols], preferred_element_type=F32)
        grad_probs = jnp.dot(value, gt[a, :, cols], preferred_element_type=F32)
        probs = jnp.exp2(scores * (SCALE * LOG2E) - norm[pl.ds(h, 1), rows] * LOG2E)
        if diagonal:
            key_at = lax.broadcasted_iota(jnp.int32, (size, size), 0)
            query_at = lax.broadcasted_iota(jnp.int32, (size, size), 1)
            probs = jnp.where(key_at <= query_at, probs, 0.0)
        grad_scores = (probs * (grad_probs - delta[pl.ds(h, 1), rows])).astype(BF16)
        dv[b] += jnp.dot(probs.astype(BF16), g[rows, lanes], preferred_element_type=F32)
        dk[b] += jnp.dot(grad_scores, q[rows, lanes], preferred_element_type=F32)
        dqt[a, :, cols] += jnp.dot(key_t, grad_scores, preferred_element_type=F32)


def own_kernel(order, q, g, o, k, v, norm, qt, gt, delta, dqt, dk, dv):
    me = lax.axis_index("ctx")
    size = q.shape[0] // 2
    heads = norm.shape[0]
    dqt[...] = jnp.zeros_like(dqt)
    dk[...] = jnp.zeros_like(dk)
    dv[...] = jnp.zeros_like(dv)
    for a in range(2):
        rows = pl.ds(a * size, size)
        for h in range(heads):
            lanes = pl.ds(h * HD, HD)
            cols = pl.ds(h * size, size)
            qt[a, :, cols] = q[rows, lanes].T
            grad = g[rows, lanes]
            gt[a, :, cols] = grad.T
            prod = grad.astype(F32) * o[rows, lanes].astype(F32)
            delta[pl.ds(h, 1), rows] = jnp.sum(prod.T, axis=0, keepdims=True)
    for b in range(2):
        rows = pl.ds(b * size, size)
        key, value = k[rows, :], v[rows, :]
        key_t = key.T
        for a in range(2):
            run = functools.partial(
                tile_terms, a, b, a == b, key, value, key_t, qt, q, gt, g, norm, delta, dqt, dk, dv
            )
            if a == b:
                run()
            else:
                pl.when(order[2 * me + b] < order[2 * me + a])(run)


def remote_kernel(partner, order, kv, q, g, qt, gt, norm, delta, dqt_in, dqt, part, dk, dv):
    me = lax.axis_index("ctx")
    other = partner(me)
    size = q.shape[0] // 2
    dqt[...] = dqt_in[...]
    dk[...] = jnp.zeros_like(dk)
    dv[...] = jnp.zeros_like(dv)
    for b in range(2):
        key = kv[pl.ds(b * size, size), :]
        value = kv[pl.ds((2 + b) * size, size), :]
        key_t = key.T
        for a in range(2):
            run = functools.partial(
                tile_terms, a, b, False, key, value, key_t, qt, q, gt, g, norm, delta, dqt, dk, dv
            )
            pl.when(order[2 * other + b] < order[2 * me + a])(run)
        part[pl.ds(b * size, size), :] = (dk[b] * SCALE).astype(BF16)
        part[pl.ds((2 + b) * size, size), :] = dv[b].astype(BF16)


def queries_kernel(dqt, dq):
    size = dq.shape[0] // 2
    for a in range(2):
        for h in range(dq.shape[1] // HD):
            tile = dqt[a, :, pl.ds(h * size, size)] * SCALE
            dq[pl.ds(a * size, size), pl.ds(h * HD, HD)] = tile.T.astype(BF16)


def sums_kernel(dk, dv, *refs):
    parts, (out_k, out_v) = refs[:-2], refs[-2:]
    size = dk.shape[1]
    for b in range(2):
        rows = pl.ds(b * size, size)
        key_sum, value_sum = dk[b] * SCALE, dv[b]
        for part in parts:
            key_sum += part[rows, :].astype(F32)
            value_sum += part[pl.ds((2 + b) * size, size), :].astype(F32)
        out_k[rows, :] = key_sum.astype(BF16)
        out_v[rows, :] = value_sum.astype(BF16)


SMEM = pl.BlockSpec(memory_space=pltpu.SMEM)
VMEM = pl.BlockSpec(memory_space=pltpu.VMEM)


def call(body, outs, n_in, smem=0, scratch=(), aliases=None, flops=0, moved=0):
    return pl.pallas_call(
        body,
        out_shape=[jax.ShapeDtypeStruct(s, t) for s, t in outs],
        in_specs=[SMEM] * smem + [VMEM] * (n_in - smem),
        out_specs=[VMEM] * len(outs),
        scratch_shapes=list(scratch),
        input_output_aliases=aliases or {},
        compiler_params=pltpu.CompilerParams(vmem_limit_bytes=VMEM_LIMIT),
        cost_estimate=pl.CostEstimate(flops=flops, bytes_accessed=moved, transcendentals=0),
    )


def partner_of(n, s):
    if n & (n - 1) == 0:
        return lambda i: i ^ s
    return lambda i: lax.rem(i + n - s, n) if not isinstance(i, int) else (i + n - s) % n


def shards(n, queries, keys, values, outputs, out_grads, log_norms, stretch_order):
    rows = queries.shape[0]
    size = rows // 2
    heads = queries.shape[1] // HD
    work = 5 * 2 * rows * rows * heads * HD
    kv = jnp.concatenate([keys, values], axis=0)
    partners = [partner_of(n, s) for s in range(1, n)]
    arrived = [lax.ppermute(kv, "ctx", [(p(i), i) for i in range(n)]) for p in partners]
    wide = (2, HD, heads * size)
    qt, gt, delta, dqt, dk, dv = call(
        own_kernel,
        [(wide, BF16), (wide, BF16), ((heads, rows), F32), (wide, F32), ((2, size, HD), F32), ((2, size, HD), F32)],
        7,
        smem=1,
        flops=work,
        moved=8 * rows * heads * HD,
    )(stretch_order, queries, out_grads, outputs, keys, values, log_norms)
    returned = []
    for p, got in zip(partners, arrived):
        dqt, part = call(
            functools.partial(remote_kernel, p),
            [(wide, F32), ((4 * size, HD), BF16)],
            9,
            smem=1,
            scratch=[pltpu.VMEM((2, size, HD), F32)] * 2,
            aliases={8: 0},
            flops=work,
            moved=8 * rows * heads * HD,
        )(stretch_order, got, queries, out_grads, qt, gt, log_norms, delta, dqt)
        returned.append(lax.ppermute(part, "ctx", [(i, p(i)) for i in range(n)]))
    (grad_queries,) = call(queries_kernel, [(queries.shape, BF16)], 1, moved=6 * rows * heads * HD)(dqt)
    grad_keys, grad_values = call(sums_kernel, [(keys.shape, BF16), (values.shape, BF16)], 2 + len(returned), moved=16 * rows * HD)(
        dk, dv, *returned
    )
    return grad_queries, grad_keys, grad_values


def solution(mesh):
    return jax.shard_map(
        functools.partial(shards, mesh.shape["ctx"]),
        mesh=mesh,
        in_specs=(
            P(("dp", "ctx"), "tp"),
            P(("dp", "ctx"), "tp"),
            P(("dp", "ctx"), "tp"),
            P(("dp", "ctx"), "tp"),
            P(("dp", "ctx"), "tp"),
            P("tp", ("dp", "ctx")),
            P("dp"),
        ),
        out_specs=(P(("dp", "ctx"), "tp"), P(("dp", "ctx"), "tp"), P(("dp", "ctx"), "tp")),
        check_vma=False,
    )
```

```python
import functools
import math

import jax
import jax.numpy as jnp
from jax import lax
from jax.experimental import pallas as pl
from jax.experimental.pallas import tpu as pltpu
from jax.sharding import PartitionSpec as P

HD = 128
SCALE = HD ** (-0.5)
LOG2E = math.log2(math.e)
F32 = jnp.float32
BF16 = jnp.bfloat16
VMEM_LIMIT = 48 * 1024 * 1024


def tile_terms(a, b, diagonal, key, value, key_t, qt, q, gt, g, norm, delta, dqt, dk, dv):
    size = key.shape[0]
    heads = norm.shape[0]
    for h in range(heads):
        cols = pl.ds(h * size, size)
        rows = pl.ds(a * size, size)
        lanes = pl.ds(h * HD, HD)
        scores = jnp.dot(key, qt[a, :, cols], preferred_element_type=F32)
        grad_probs = jnp.dot(value, gt[a, :, cols], preferred_element_type=F32)
        probs = jnp.exp2(scores * (SCALE * LOG2E) - norm[pl.ds(h, 1), rows] * LOG2E)
        if diagonal:
            key_at = lax.broadcasted_iota(jnp.int32, (size, size), 0)
            query_at = lax.broadcasted_iota(jnp.int32, (size, size), 1)
            probs = jnp.where(key_at <= query_at, probs, 0.0)
        grad_scores = (probs * (grad_probs - delta[pl.ds(h, 1), rows])).astype(BF16)
        dv[b] += jnp.dot(probs.astype(BF16), g[rows, lanes], preferred_element_type=F32)
        dk[b] += jnp.dot(grad_scores, q[rows, lanes], preferred_element_type=F32)
        dqt[a, :, cols] += jnp.dot(key_t, grad_scores, preferred_element_type=F32)


def own_kernel(order, kv, norm, q_hbm, g_hbm, o_hbm, q, g, qt, gt, delta, dqt, dk, dv, o, sems):
    me = lax.axis_index("ctx")
    size = q.shape[0] // 2
    heads = norm.shape[0]
    loads = [
        pltpu.make_async_copy(src, dst, sems.at[i])
        for i, (src, dst) in enumerate(((q_hbm, q), (g_hbm, g), (o_hbm, o)))
    ]
    for load in loads:
        load.start()
    dqt[...] = jnp.zeros_like(dqt)
    dk[...] = jnp.zeros_like(dk)
    dv[...] = jnp.zeros_like(dv)
    for load in loads:
        load.wait()
    for a in range(2):
        rows = pl.ds(a * size, size)
        for h in range(heads):
            lanes = pl.ds(h * HD, HD)
            cols = pl.ds(h * size, size)
            qt[a, :, cols] = q[rows, lanes].T
            grad = g[rows, lanes]
            gt[a, :, cols] = grad.T
            prod = grad.astype(F32) * o[rows, lanes].astype(F32)
            delta[pl.ds(h, 1), rows] = jnp.sum(prod.T, axis=0, keepdims=True)
    for b in range(2):
        key = kv[pl.ds(b * size, size), :]
        value = kv[pl.ds((2 + b) * size, size), :]
        key_t = key.T
        for a in range(2):
            run = functools.partial(
                tile_terms, a, b, a == b, key, value, key_t, qt, q, gt, g, norm, delta, dqt, dk, dv
            )
            if a == b:
                run()
            else:
                pl.when(order[2 * me + b] < order[2 * me + a])(run)
        dk[b] *= SCALE


def remote_kernel(partner, order, kv, q, g, qt, gt, norm, delta, dqt_in, dqt, part, dk, dv):
    me = lax.axis_index("ctx")
    other = partner(me)
    size = q.shape[0] // 2
    dqt[...] = dqt_in[...]
    dk[...] = jnp.zeros_like(dk)
    dv[...] = jnp.zeros_like(dv)
    for b in range(2):
        key = kv[pl.ds(b * size, size), :]
        value = kv[pl.ds((2 + b) * size, size), :]
        key_t = key.T
        for a in range(2):
            run = functools.partial(
                tile_terms, a, b, False, key, value, key_t, qt, q, gt, g, norm, delta, dqt, dk, dv
            )
            pl.when(order[2 * other + b] < order[2 * me + a])(run)
        part[pl.ds(b * size, size), :] = (dk[b] * SCALE).astype(BF16)
        part[pl.ds((2 + b) * size, size), :] = dv[b].astype(BF16)


def queries_kernel(dqt, dq):
    size = dq.shape[0] // 2
    for a in range(2):
        for h in range(dq.shape[1] // HD):
            tile = dqt[a, :, pl.ds(h * size, size)] * SCALE
            dq[pl.ds(a * size, size), pl.ds(h * HD, HD)] = tile.T.astype(BF16)


def sums_kernel(dk, dv, *refs):
    parts, (out_k, out_v) = refs[:-2], refs[-2:]
    size = dk.shape[1]
    for b in range(2):
        key_sum, value_sum = dk[b], dv[b]
        for part in parts:
            key_sum += part[pl.ds(b * size, size), :].astype(F32)
            value_sum += part[pl.ds((2 + b) * size, size), :].astype(F32)
        if len(out_k.shape) == 3:
            out_k[b] = key_sum
            out_v[b] = value_sum
        else:
            out_k[pl.ds(b * size, size), :] = key_sum.astype(BF16)
            out_v[pl.ds(b * size, size), :] = value_sum.astype(BF16)


def token_kernel(x, *refs):
    pass


SMEM = pl.BlockSpec(memory_space=pltpu.SMEM)
VMEM = pl.BlockSpec(memory_space=pltpu.VMEM)
ANY = pl.BlockSpec(memory_space=pl.ANY)
HBM = pl.BlockSpec(memory_space=pltpu.HBM)


def call(body, outs, in_specs, out_spec=VMEM, scratch=(), aliases=None, flops=0, moved=0):
    return pl.pallas_call(
        body,
        out_shape=[jax.ShapeDtypeStruct(s, t) for s, t in outs],
        in_specs=in_specs,
        out_specs=[out_spec] * len(outs),
        scratch_shapes=list(scratch),
        input_output_aliases=aliases or {},
        compiler_params=pltpu.CompilerParams(vmem_limit_bytes=VMEM_LIMIT),
        cost_estimate=pl.CostEstimate(flops=flops, bytes_accessed=moved, transcendentals=0),
    )


def after(x, *others):
    return call(token_kernel, [(x.shape, x.dtype)], [ANY] * (1 + len(others)), out_spec=ANY, aliases={0: 0})(x, *others)[0]


def partner_of(n, s):
    if n & (n - 1) == 0:
        return lambda i: i ^ s
    return lambda i: lax.rem(i + n - s, n) if not isinstance(i, int) else (i + n - s) % n


def shards(n, queries, keys, values, outputs, out_grads, log_norms, stretch_order):
    rows = queries.shape[0]
    size = rows // 2
    heads = queries.shape[1] // HD
    work = 5 * 2 * rows * rows * heads * HD
    kv = jnp.concatenate([keys, values], axis=0)
    wide = (2, HD, heads * size)
    part_type = ((4 * size, HD), BF16)
    sums_type = ((2, size, HD), F32)

    def send(x, pairs):
        return lax.ppermute(x, "ctx", pairs)

    def own():
        return call(
            own_kernel,
            [(queries.shape, BF16), (queries.shape, BF16), (wide, BF16), (wide, BF16),
             ((heads, rows), F32), (wide, F32), sums_type, sums_type],
            [SMEM, VMEM, VMEM, HBM, HBM, HBM],
            scratch=[pltpu.VMEM(queries.shape, BF16), pltpu.SemaphoreType.DMA((3,))],
            flops=work,
        )(stretch_order, kv, log_norms, queries, out_grads, outputs)

    def remote(partner, kv, q, g, qt, gt, delta, dqt):
        return call(
            functools.partial(remote_kernel, partner),
            [(wide, F32), part_type],
            [SMEM] + [VMEM] * 8,
            scratch=[pltpu.VMEM((2, size, HD), F32)] * 2,
            aliases={8: 0},
            flops=work,
        )(stretch_order, kv, q, g, qt, gt, log_norms, delta, dqt)

    def sums(dk, dv, parts, outs):
        return call(sums_kernel, outs, [VMEM] * (2 + len(parts)), moved=16 * rows * HD)(dk, dv, *parts)

    last = [(keys.shape, BF16), (values.shape, BF16)]
    if n == 4:
        swap = [[(i, i ^ s) for i in range(n)] for s in range(n)]
        kv_3 = send(kv, swap[3])
        kv_1 = send(kv, swap[1])
        q, g, qt, gt, delta, dqt, dk, dv = own()
        same = (q, g, qt, gt, delta)
        dqt, part_1 = remote(lambda i: i ^ 1, kv_1, *same, dqt)
        back_1 = send(part_1, swap[1])
        kv_3 = after(kv_3, part_1)
        kv_2 = send(kv_3, swap[1])
        dqt, part_3 = remote(lambda i: i ^ 3, kv_3, *same, dqt)
        back_3 = send(part_3, swap[3])
        dqt, part_2 = remote(lambda i: i ^ 2, kv_2, *same, dqt)
        back_2 = send(part_2, swap[2])
        dk, dv = sums(dk, dv, [back_1, back_3], [sums_type] * 2)
        returned = [back_2]
    else:
        partners = [partner_of(n, s) for s in range(1, n)]
        arrived = [send(kv, [(p(i), i) for i in range(n)]) for p in partners]
        q, g, qt, gt, delta, dqt, dk, dv = own()
        returned = []
        for p, got in zip(partners, arrived):
            dqt, part = remote(p, got, q, g, qt, gt, delta, dqt)
            returned.append(send(part, [(i, p(i)) for i in range(n)]))
    (grad_queries,) = call(queries_kernel, [(queries.shape, BF16)], [VMEM])(dqt)
    grad_keys, grad_values = sums(dk, dv, returned, last)
    return grad_queries, grad_keys, grad_values


def solution(mesh):
    return jax.shard_map(
        functools.partial(shards, mesh.shape["ctx"]),
        mesh=mesh,
        in_specs=(
            P(("dp", "ctx"), "tp"),
            P(("dp", "ctx"), "tp"),
            P(("dp", "ctx"), "tp"),
            P(("dp", "ctx"), "tp"),
            P(("dp", "ctx"), "tp"),
            P("tp", ("dp", "ctx")),
            P("dp"),
        ),
        out_specs=(P(("dp", "ctx"), "tp"), P(("dp", "ctx"), "tp"), P(("dp", "ctx"), "tp")),
        check_vma=False,
    )
```

```python
import functools
import math

import jax
import jax.numpy as jnp
from jax import lax
from jax.experimental import pallas as pl
from jax.experimental.pallas import tpu as pltpu
from jax.sharding import PartitionSpec as P

HD = 128
SCALE = HD ** (-0.5)
LOG2E = math.log2(math.e)
F32 = jnp.float32
BF16 = jnp.bfloat16
VMEM_LIMIT = 48 * 1024 * 1024


def low_terms(start, width, key, value, state, diagonal, ps, ds):
    _, _, qt, gt, norm, delta = state
    size = key.shape[0]
    for at in range(0, width, size):
        cols = pl.ds(start + at, size)
        scores = jnp.dot(key, qt[:, cols], preferred_element_type=F32)
        grad_probs = jnp.dot(value, gt[:, cols], preferred_element_type=F32)
        probs = jnp.exp2(scores * (SCALE * LOG2E) - norm[:, cols])
        if diagonal:
            key_at = lax.broadcasted_iota(jnp.int32, probs.shape, 0)
            query_at = lax.broadcasted_iota(jnp.int32, probs.shape, 1)
            probs = jnp.where(key_at <= query_at, probs, 0.0)
        ps[:, at : at + size] = probs.astype(BF16)
        ds[:, at : at + size] = (probs * (grad_probs - delta[:, cols])).astype(BF16)


def key_terms(start, width, state, ps, ds):
    q4, g4 = state[:2]
    rows = pl.ds(start, width)
    grad_key = jnp.dot(ds[:, :width], q4[rows, :], preferred_element_type=F32)
    grad_value = jnp.dot(ps[:, :width], g4[rows, :], preferred_element_type=F32)
    return grad_key * SCALE, grad_value


def own_kernel(order, kv, log_norms, q, g, o, kv_out, q4, g4, qt, gt, norm, delta, dqt, dk, dv, ps, ds):
    me = lax.axis_index("ctx")
    size = q.shape[0] // 2
    heads = log_norms.shape[0]
    width = heads * size
    kv_out[...] = kv[...]
    for a in range(2):
        rows = pl.ds(a * size, size)
        for h in range(heads):
            lanes = pl.ds(h * HD, HD)
            cols = pl.ds(a * width + h * size, size)
            query, grad = q[rows, lanes], g[rows, lanes]
            q4[cols, :] = query
            g4[cols, :] = grad
            qt[:, cols] = query.T
            gt[:, cols] = grad.T
            prod = grad.astype(F32) * o[rows, lanes].astype(F32)
            delta[:, cols] = jnp.sum(prod.T, axis=0, keepdims=True)
            norm[:, cols] = log_norms[pl.ds(h, 1), rows] * LOG2E
    state = (q4, g4, qt, gt, norm, delta)
    for a in range(2):
        key, value = kv[pl.ds(2 * a * size, size), :], kv[pl.ds((2 * a + 1) * size, size), :]
        rows, cols = pl.ds(a * size, size), pl.ds(a * width, width)
        low_terms(a * width, width, key, value, state, True, ps, ds)
        dk[rows, :], dv[rows, :] = key_terms(a * width, width, state, ps, ds)
        dqt[:, cols] = jnp.dot(key.T, ds[...], preferred_element_type=F32)
    late = (order[2 * me] < order[2 * me + 1]).astype(jnp.int32)
    start = pl.multiple_of(late * width, width)
    key_at = pl.multiple_of((1 - late) * 2 * size, size)
    key, value = kv[pl.ds(key_at, size), :], kv[pl.ds(key_at + size, size), :]
    low_terms(start, width, key, value, state, False, ps, ds)
    rows = pl.ds(pl.multiple_of((1 - late) * size, size), size)
    grad_key, grad_value = key_terms(start, width, state, ps, ds)
    dk[rows, :] += grad_key
    dv[rows, :] += grad_value
    dqt[:, pl.ds(start, width)] += jnp.dot(key.T, ds[...], preferred_element_type=F32)


def remote_kernel(partner, first, order, kv, q4, g4, qt, gt, norm, delta, dqt_in, dqt, part, ps, ds):
    me = lax.axis_index("ctx")
    other = partner(me)
    total = q4.shape[0]
    width = total // 2
    size = ps.shape[0]
    state = (q4, g4, qt, gt, norm, delta)
    for b in range(kv.shape[0] // (2 * size)):
        keys_at, values_at = pl.ds(2 * b * size, size), pl.ds((2 * b + 1) * size, size)
        before = dqt_in if b == 0 else dqt
        sees = [order[2 * other + first + b] < order[2 * me + a] for a in range(2)]
        count = sees[0].astype(jnp.int32) + sees[1].astype(jnp.int32)

        def some(start, span):
            key, value = kv[keys_at, :], kv[values_at, :]
            low_terms(start, span, key, value, state, False, ps, ds)
            grad_key, grad_value = key_terms(start, span, state, ps, ds)
            part[keys_at, :] = grad_key.astype(BF16)
            part[values_at, :] = grad_value.astype(BF16)
            cols = pl.ds(start, span)
            dqt[:, cols] = before[:, cols] + jnp.dot(key.T, ds[:, :span], preferred_element_type=F32)

        @pl.when(count == 2)
        def _():
            some(0, total)

        @pl.when(count == 1)
        def _():
            seeing = sees[1].astype(jnp.int32)
            some(pl.multiple_of(seeing * width, width), width)
            if b == 0:
                rest = pl.ds(pl.multiple_of((1 - seeing) * width, width), width)
                dqt[:, rest] = dqt_in[:, rest]

        @pl.when(count == 0)
        def _():
            part[keys_at, :] = jnp.zeros((size, HD), BF16)
            part[values_at, :] = jnp.zeros((size, HD), BF16)
            if b == 0:
                dqt[...] = dqt_in[...]


def queries_kernel(dqt, dq):
    size = dq.shape[0] // 2
    heads = dq.shape[1] // HD
    for a in range(2):
        for h in range(heads):
            tile = dqt[:, pl.ds((a * heads + h) * size, size)] * SCALE
            dq[pl.ds(a * size, size), pl.ds(h * HD, HD)] = tile.T.astype(BF16)


def sums_kernel(dk, dv, *refs):
    parts, (out_k, out_v) = refs[:-2], refs[-2:]
    size = dk.shape[0] // 2
    for b in range(2):
        rows = pl.ds(b * size, size)
        key_sum, value_sum = dk[rows, :], dv[rows, :]
        for part in parts:
            key_sum += part[pl.ds(2 * b * size, size), :].astype(F32)
            value_sum += part[pl.ds((2 * b + 1) * size, size), :].astype(F32)
        out_k[rows, :] = key_sum.astype(out_k.dtype)
        out_v[rows, :] = value_sum.astype(out_v.dtype)


def token_kernel(x, *refs):
    pass


SMEM = pl.BlockSpec(memory_space=pltpu.SMEM)
VMEM = pl.BlockSpec(memory_space=pltpu.VMEM)
ANY = pl.BlockSpec(memory_space=pl.ANY)


def call(body, outs, in_specs, out_spec=VMEM, scratch=(), aliases=None, flops=0, moved=0):
    return pl.pallas_call(
        body,
        out_shape=[jax.ShapeDtypeStruct(s, t) for s, t in outs],
        in_specs=in_specs,
        out_specs=[out_spec] * len(outs),
        scratch_shapes=list(scratch),
        input_output_aliases=aliases or {},
        compiler_params=pltpu.CompilerParams(vmem_limit_bytes=VMEM_LIMIT),
        cost_estimate=pl.CostEstimate(flops=flops, bytes_accessed=moved, transcendentals=0),
    )


def after(x, *others):
    return call(token_kernel, [(x.shape, x.dtype)], [ANY] * (1 + len(others)), out_spec=ANY, aliases={0: 0})(x, *others)[0]


def partner_of(n, s):
    if n & (n - 1) == 0:
        return lambda i: i ^ s
    return lambda i: lax.rem(i + n - s, n) if not isinstance(i, int) else (i + n - s) % n


def shards(n, queries, keys, values, outputs, out_grads, log_norms, stretch_order):
    rows = queries.shape[0]
    size = rows // 2
    heads = queries.shape[1] // HD
    work = 5 * 2 * rows * rows * heads * HD
    total = 2 * heads * size
    wide = (HD, total)
    tall = (total, HD)
    line = (1, total)
    whole_type = ((4 * size, HD), BF16)
    sums_type = ((rows, HD), F32)

    def send(x, pairs):
        return lax.ppermute(x, "ctx", pairs)

    def own(kv):
        return call(
            own_kernel,
            [whole_type, (tall, BF16), (tall, BF16), (wide, BF16), (wide, BF16), (line, F32), (line, F32), (wide, F32), sums_type, sums_type],
            [SMEM] + [VMEM] * 5,
            scratch=[pltpu.VMEM((size, heads * size), BF16)] * 2,
            flops=work,
        )(stretch_order, kv, log_norms, queries, out_grads, outputs)

    def remote(partner, first, kv, *state):
        return call(
            functools.partial(remote_kernel, partner, first),
            [(wide, F32), (kv.shape, BF16)],
            [SMEM] + [VMEM] * 8,
            scratch=[pltpu.VMEM((size, total), BF16)] * 2,
            aliases={8: 0},
            flops=work * kv.shape[0] // (4 * size),
        )(stretch_order, kv, *state)

    def sums(dk, dv, parts, outs):
        return call(sums_kernel, outs, [VMEM] * (2 + len(parts)), moved=16 * rows * HD)(dk, dv, *parts)

    last = [(keys.shape, BF16), (values.shape, BF16)]
    kv = jnp.concatenate([keys[:size], values[:size], keys[size:], values[size:]], axis=0)
    if n == 4:
        swap = [[(i, i ^ s) for i in range(n)] for s in range(n)]
        kv_3 = send(kv, swap[3])
        kv, *same, dqt, dk, dv = own(kv)
        kv_1 = send(kv, swap[1])
        kv_3 = after(kv_3, dk)
        kv_2 = send(kv_3, swap[1])
        dqt, part_3 = remote(lambda i: i ^ 3, 0, kv_3, *same, dqt)
        back_3 = send(part_3, swap[3])
        kv_1 = after(kv_1, part_3)
        dqt, part_1 = remote(lambda i: i ^ 1, 0, kv_1, *same, dqt)
        back_1 = send(part_1, swap[1])
        dqt, part_2 = remote(lambda i: i ^ 2, 0, kv_2, *same, dqt)
        back_2 = send(part_2, swap[2])
        dk, dv = sums(dk, dv, [back_3, back_1], [sums_type] * 2)
        returned = [back_2]
    else:
        kv, *same, dqt, dk, dv = own(kv)
        partners = [partner_of(n, s) for s in range(1, n)]
        arrived = [send(kv, [(p(i), i) for i in range(n)]) for p in partners]
        returned = []
        for p, got in zip(partners, arrived):
            dqt, part = remote(p, 0, got, *same, dqt)
            returned.append(send(part, [(i, p(i)) for i in range(n)]))
    (grad_queries,) = call(queries_kernel, [(queries.shape, BF16)], [VMEM])(dqt)
    grad_keys, grad_values = sums(dk, dv, returned, last)
    return grad_queries, grad_keys, grad_values


def solution(mesh):
    return jax.shard_map(
        functools.partial(shards, mesh.shape["ctx"]),
        mesh=mesh,
        in_specs=(
            P(("dp", "ctx"), "tp"),
            P(("dp", "ctx"), "tp"),
            P(("dp", "ctx"), "tp"),
            P(("dp", "ctx"), "tp"),
            P(("dp", "ctx"), "tp"),
            P("tp", ("dp", "ctx")),
            P("dp"),
        ),
        out_specs=(P(("dp", "ctx"), "tp"), P(("dp", "ctx"), "tp"), P(("dp", "ctx"), "tp")),
        check_vma=False,
    )
```

```python
import functools
import math

import jax
import jax.numpy as jnp
from jax import lax
from jax.experimental import pallas as pl
from jax.experimental.pallas import tpu as pltpu
from jax.sharding import PartitionSpec as P

HD = 128
SCALE = HD ** (-0.5)
WEIGHT = 10
LOG2E = math.log2(math.e)
F32 = jnp.float32
BF16 = jnp.bfloat16
VMEM_LIMIT = 48 * 1024 * 1024


def low_terms(start, width, key, value, state, diagonal, ps, ds):
    _, _, qt, gt, norm, delta = state
    size = key.shape[0]
    for at in range(0, width, size):
        cols = pl.ds(start + at, size)
        scores = jnp.dot(key, qt[:, cols], preferred_element_type=F32)
        grad_probs = jnp.dot(value, gt[:, cols], preferred_element_type=F32)
        probs = jnp.exp2(scores * (SCALE * LOG2E) - norm[:, cols])
        if diagonal:
            key_at = lax.broadcasted_iota(jnp.int32, probs.shape, 0)
            query_at = lax.broadcasted_iota(jnp.int32, probs.shape, 1)
            probs = jnp.where(key_at <= query_at, probs, 0.0)
        ps[:, at : at + size] = probs.astype(BF16)
        ds[:, at : at + size] = (probs * (grad_probs - delta[:, cols])).astype(BF16)


def key_terms(start, width, state, ps, ds):
    q4, g4 = state[:2]
    rows = pl.ds(start, width)
    grad_key = jnp.dot(ds[:, :width], q4[rows, :], preferred_element_type=F32)
    grad_value = jnp.dot(ps[:, :width], g4[rows, :], preferred_element_type=F32)
    return grad_key * SCALE, grad_value


def prepare_kernel(log_norms, q, g, o, q4, g4, qt, gt, norm, delta):
    size = q.shape[0] // 2
    heads = log_norms.shape[0]
    width = heads * size
    for a in range(2):
        rows = pl.ds(a * size, size)
        for h in range(heads):
            lanes = pl.ds(h * HD, HD)
            cols = pl.ds(a * width + h * size, size)
            query, grad = q[rows, lanes], g[rows, lanes]
            q4[cols, :] = query
            g4[cols, :] = grad
            qt[:, cols] = query.T
            gt[:, cols] = grad.T
            prod = grad.astype(F32) * o[rows, lanes].astype(F32)
            delta[:, cols] = jnp.sum(prod.T, axis=0, keepdims=True)
            norm[:, cols] = log_norms[pl.ds(h, 1), rows] * LOG2E


def own_kernel(order, k, v, q4, g4, qt, gt, norm, delta, dqt, dk, dv, ps, ds):
    me = lax.axis_index("ctx")
    size, width = ps.shape
    state = (q4, g4, qt, gt, norm, delta)
    for a in range(2):
        rows, cols = pl.ds(a * size, size), pl.ds(a * width, width)
        key, value = k[rows, :], v[rows, :]
        low_terms(a * width, width, key, value, state, True, ps, ds)
        dk[rows, :], dv[rows, :] = key_terms(a * width, width, state, ps, ds)
        dqt[:, cols] = jnp.dot(key.T, ds[...], preferred_element_type=F32)
    late = (order[2 * me] < order[2 * me + 1]).astype(jnp.int32)
    start = pl.multiple_of(late * width, width)
    rows = pl.ds(pl.multiple_of((1 - late) * size, size), size)
    key, value = k[rows, :], v[rows, :]
    low_terms(start, width, key, value, state, False, ps, ds)
    grad_key, grad_value = key_terms(start, width, state, ps, ds)
    dk[rows, :] += grad_key
    dv[rows, :] += grad_value
    dqt[:, pl.ds(start, width)] += jnp.dot(key.T, ds[...], preferred_element_type=F32)


def remote_kernel(partner, order, k, v, q4, g4, qt, gt, norm, delta, dqt_in, dqt, part, ps, ds):
    me = lax.axis_index("ctx")
    other = partner(me)
    total = q4.shape[0]
    width = total // 2
    size = ps.shape[0]
    state = (q4, g4, qt, gt, norm, delta)
    for b in range(2):
        rows, values_to = pl.ds(b * size, size), pl.ds((2 + b) * size, size)
        before = dqt_in if b == 0 else dqt
        sees = [order[2 * other + b] < order[2 * me + a] for a in range(2)]
        count = sees[0].astype(jnp.int32) + sees[1].astype(jnp.int32)

        def some(start, span):
            key, value = k[rows, :], v[rows, :]
            low_terms(start, span, key, value, state, False, ps, ds)
            grad_key, grad_value = key_terms(start, span, state, ps, ds)
            part[rows, :] = grad_key.astype(BF16)
            part[values_to, :] = grad_value.astype(BF16)
            cols = pl.ds(start, span)
            dqt[:, cols] = before[:, cols] + jnp.dot(key.T, ds[:, :span], preferred_element_type=F32)

        @pl.when(count == 2)
        def _():
            some(0, total)

        @pl.when(count == 1)
        def _():
            seeing = sees[1].astype(jnp.int32)
            some(pl.multiple_of(seeing * width, width), width)
            if b == 0:
                rest = pl.ds(pl.multiple_of((1 - seeing) * width, width), width)
                dqt[:, rest] = dqt_in[:, rest]

        @pl.when(count == 0)
        def _():
            part[rows, :] = jnp.zeros((size, HD), BF16)
            part[values_to, :] = jnp.zeros((size, HD), BF16)
            if b == 0:
                dqt[...] = dqt_in[...]


def queries_kernel(dqt, dq):
    size = dq.shape[0] // 2
    heads = dq.shape[1] // HD
    for a in range(2):
        for h in range(heads):
            tile = dqt[:, pl.ds((a * heads + h) * size, size)] * SCALE
            dq[pl.ds(a * size, size), pl.ds(h * HD, HD)] = tile.T.astype(BF16)


def sums_kernel(dk, dv, *refs):
    parts, (out_k, out_v) = refs[:-2], refs[-2:]
    rows = dk.shape[0]
    key_sum, value_sum = dk[...], dv[...]
    for part in parts:
        key_sum += part[:rows, :].astype(F32)
        value_sum += part[rows:, :].astype(F32)
    out_k[...] = key_sum.astype(out_k.dtype)
    out_v[...] = value_sum.astype(out_v.dtype)


def add_kernel(first, second, both):
    both[...] = (first[...].astype(F32) + second[...].astype(F32)).astype(BF16)


def token_kernel(x, *refs):
    pass


SMEM = pl.BlockSpec(memory_space=pltpu.SMEM)
VMEM = pl.BlockSpec(memory_space=pltpu.VMEM)
ANY = pl.BlockSpec(memory_space=pl.ANY)


def call(body, outs, in_specs, out_spec=VMEM, scratch=(), aliases=None, flops=0, moved=0):
    return pl.pallas_call(
        body,
        out_shape=[jax.ShapeDtypeStruct(s, t) for s, t in outs],
        in_specs=in_specs,
        out_specs=[out_spec] * len(outs),
        scratch_shapes=list(scratch),
        input_output_aliases=aliases or {},
        compiler_params=pltpu.CompilerParams(vmem_limit_bytes=VMEM_LIMIT),
        cost_estimate=pl.CostEstimate(flops=flops, bytes_accessed=moved, transcendentals=0),
    )


def after(x, *others):
    return call(token_kernel, [(x.shape, x.dtype)], [ANY] * (1 + len(others)), out_spec=ANY, aliases={0: 0})(x, *others)[0]


def partner_of(n, s):
    if n & (n - 1) == 0:
        return lambda i: i ^ s
    return lambda i: lax.rem(i + n - s, n) if not isinstance(i, int) else (i + n - s) % n


def shards(n, queries, keys, values, outputs, out_grads, log_norms, stretch_order):
    rows = queries.shape[0]
    size = rows // 2
    heads = queries.shape[1] // HD
    work = 5 * 2 * rows * rows * heads * HD
    total = 2 * heads * size
    wide = (HD, total)
    tall = (total, HD)
    line = (1, total)
    part_type = ((4 * size, HD), BF16)
    sums_type = ((rows, HD), F32)

    def send(x, pairs):
        return lax.ppermute(x, "ctx", pairs)

    def prepare():
        return call(
            prepare_kernel,
            [(tall, BF16), (tall, BF16), (wide, BF16), (wide, BF16), (line, F32), (line, F32)],
            [VMEM] * 4,
            flops=work,
        )(log_norms, queries, out_grads, outputs)

    def own(same):
        return call(
            own_kernel,
            [(wide, F32), sums_type, sums_type],
            [SMEM] + [VMEM] * 8,
            scratch=[pltpu.VMEM((size, heads * size), BF16)] * 2,
            flops=work,
        )(stretch_order, keys, values, *same)

    def remote(s, kv, same, dqt):
        partner = s if callable(s) else lambda i: i ^ s
        return call(
            functools.partial(remote_kernel, partner),
            [(wide, F32), part_type],
            [SMEM] + [VMEM] * 9,
            scratch=[pltpu.VMEM((size, total), BF16)] * 2,
            aliases={9: 0},
            flops=WEIGHT * work,
        )(stretch_order, *kv, *same, dqt)

    def sums(dk, dv, parts, outs):
        return call(sums_kernel, outs, [VMEM] * (2 + len(parts)))(dk, dv, *parts)

    def add(first, second):
        return call(add_kernel, [part_type], [VMEM] * 2)(first, second)[0]

    last = [(keys.shape, BF16), (values.shape, BF16)]
    if n == 4:
        swap = [[(i, i ^ s) for i in range(n)] for s in range(n)]
        own_rows = (keys, values)
        kv_3 = [send(x, swap[3]) for x in own_rows]
        same = prepare()
        kv_1 = [send(x, swap[1]) for x in own_rows]
        dqt, dk, dv = own(same)
        kv_3 = [after(x, dk) for x in kv_3]
        kv_2 = [send(x, swap[1]) for x in kv_3]
        dqt, part_3 = remote(3, kv_3, same, dqt)
        aside_3 = send(part_3, swap[1])
        kv_1 = [after(x, part_3) for x in kv_1]
        dqt, part_1 = remote(1, kv_1, same, dqt)
        kv_2 = [after(x, part_1) for x in kv_2]
        dqt, part_2 = remote(2, kv_2, same, dqt)
        both = add(after(aside_3, part_2), part_2)
        back_2 = send(both, swap[2])
        back_1 = send(after(part_1, both), swap[1])
        returned = [back_1, back_2]
    else:
        same = prepare()
        dqt, dk, dv = own(same)
        partners = [partner_of(n, s) for s in range(1, n)]
        arrived = [[send(x, [(p(i), i) for i in range(n)]) for x in (keys, values)] for p in partners]
        returned = []
        for p, got in zip(partners, arrived):
            dqt, part = remote(p, got, same, dqt)
            returned.append(send(part, [(i, p(i)) for i in range(n)]))
    (grad_queries,) = call(queries_kernel, [(queries.shape, BF16)], [VMEM], flops=WEIGHT * work)(dqt)
    grad_keys, grad_values = sums(dk, dv, returned, last)
    return grad_queries, grad_keys, grad_values


def solution(mesh):
    return jax.shard_map(
        functools.partial(shards, mesh.shape["ctx"]),
        mesh=mesh,
        in_specs=(
            P(("dp", "ctx"), "tp"),
            P(("dp", "ctx"), "tp"),
            P(("dp", "ctx"), "tp"),
            P(("dp", "ctx"), "tp"),
            P(("dp", "ctx"), "tp"),
            P("tp", ("dp", "ctx")),
            P("dp"),
        ),
        out_specs=(P(("dp", "ctx"), "tp"), P(("dp", "ctx"), "tp"), P(("dp", "ctx"), "tp")),
        check_vma=False,
    )
```

```python
import functools
import math

import jax
import jax.numpy as jnp
from jax import lax
from jax.experimental import pallas as pl
from jax.experimental.pallas import tpu as pltpu
from jax.sharding import PartitionSpec as P

HD = 128
SCALE = HD ** (-0.5)
WEIGHT = 10
LOG2E = math.log2(math.e)
F32 = jnp.float32
BF16 = jnp.bfloat16
VMEM_LIMIT = 48 * 1024 * 1024


def low_terms(start, width, key, value, state, diagonal, ps, ds):
    _, _, qt, gt, norm, delta = state
    size = key.shape[0]
    for at in range(0, width, size):
        cols = pl.ds(start + at, size)
        scores = jnp.dot(key, qt[:, cols], preferred_element_type=F32)
        grad_probs = jnp.dot(value, gt[:, cols], preferred_element_type=F32)
        probs = jnp.exp2(scores * (SCALE * LOG2E) - norm[:, cols])
        if diagonal:
            key_at = lax.broadcasted_iota(jnp.int32, probs.shape, 0)
            query_at = lax.broadcasted_iota(jnp.int32, probs.shape, 1)
            probs = jnp.where(key_at <= query_at, probs, 0.0)
        ps[:, at : at + size] = probs.astype(BF16)
        ds[:, at : at + size] = ((probs * SCALE) * (grad_probs - delta[:, cols])).astype(BF16)


def key_terms(start, width, state, ps, ds):
    q4, g4 = state[:2]
    rows = pl.ds(start, width)
    grad_key = jnp.dot(ds[:, :width], q4[rows, :], preferred_element_type=F32)
    grad_value = jnp.dot(ps[:, :width], g4[rows, :], preferred_element_type=F32)
    return grad_key, grad_value


def prepare_kernel(log_norms, q, g, o, q4, g4, qt, gt, norm, delta):
    size = q.shape[0] // 2
    heads = log_norms.shape[0]
    width = heads * size
    for a in range(2):
        rows = pl.ds(a * size, size)
        for h in range(heads):
            lanes = pl.ds(h * HD, HD)
            cols = pl.ds(a * width + h * size, size)
            query, grad = q[rows, lanes], g[rows, lanes]
            q4[cols, :] = query
            g4[cols, :] = grad
            qt[:, cols] = query.T
            gt[:, cols] = grad.T
            prod = grad.astype(F32) * o[rows, lanes].astype(F32)
            delta[:, cols] = jnp.sum(prod.T, axis=0, keepdims=True)
            norm[:, cols] = log_norms[pl.ds(h, 1), rows] * LOG2E


def own_kernel(order, k, v, q4, g4, qt, gt, norm, delta, dqt, dk, dv, ps, ds):
    me = lax.axis_index("ctx")
    size, width = ps.shape
    state = (q4, g4, qt, gt, norm, delta)
    for a in range(2):
        rows, cols = pl.ds(a * size, size), pl.ds(a * width, width)
        key, value = k[rows, :], v[rows, :]
        low_terms(a * width, width, key, value, state, True, ps, ds)
        dk[rows, :], dv[rows, :] = key_terms(a * width, width, state, ps, ds)
        dqt[:, cols] = jnp.dot(key.T, ds[...], preferred_element_type=F32)
    late = (order[2 * me] < order[2 * me + 1]).astype(jnp.int32)
    start = pl.multiple_of(late * width, width)
    rows = pl.ds(pl.multiple_of((1 - late) * size, size), size)
    key, value = k[rows, :], v[rows, :]
    low_terms(start, width, key, value, state, False, ps, ds)
    grad_key, grad_value = key_terms(start, width, state, ps, ds)
    dk[rows, :] += grad_key
    dv[rows, :] += grad_value
    dqt[:, pl.ds(start, width)] += jnp.dot(key.T, ds[...], preferred_element_type=F32)


def remote_kernel(partner, order, k, v, q4, g4, qt, gt, norm, delta, dqt_in, dqt, part, ps, ds):
    me = lax.axis_index("ctx")
    other = partner(me)
    total = q4.shape[0]
    width = total // 2
    size = ps.shape[0]
    state = (q4, g4, qt, gt, norm, delta)
    for b in range(2):
        rows, values_to = pl.ds(b * size, size), pl.ds((2 + b) * size, size)
        before = dqt_in if b == 0 else dqt
        sees = [order[2 * other + b] < order[2 * me + a] for a in range(2)]
        count = sees[0].astype(jnp.int32) + sees[1].astype(jnp.int32)

        def some(start, span):
            key, value = k[rows, :], v[rows, :]
            low_terms(start, span, key, value, state, False, ps, ds)
            grad_key, grad_value = key_terms(start, span, state, ps, ds)
            part[rows, :] = grad_key.astype(BF16)
            part[values_to, :] = grad_value.astype(BF16)
            cols = pl.ds(start, span)
            dqt[:, cols] = before[:, cols] + jnp.dot(key.T, ds[:, :span], preferred_element_type=F32)

        @pl.when(count == 2)
        def _():
            some(0, total)

        @pl.when(count == 1)
        def _():
            seeing = sees[1].astype(jnp.int32)
            some(pl.multiple_of(seeing * width, width), width)
            if b == 0:
                rest = pl.ds(pl.multiple_of((1 - seeing) * width, width), width)
                dqt[:, rest] = dqt_in[:, rest]

        @pl.when(count == 0)
        def _():
            part[rows, :] = jnp.zeros((size, HD), BF16)
            part[values_to, :] = jnp.zeros((size, HD), BF16)
            if b == 0:
                dqt[...] = dqt_in[...]


def queries_kernel(dqt, dq):
    size = dq.shape[0] // 2
    heads = dq.shape[1] // HD
    for a in range(2):
        for h in range(heads):
            tile = dqt[:, pl.ds((a * heads + h) * size, size)]
            dq[pl.ds(a * size, size), pl.ds(h * HD, HD)] = tile.T.astype(BF16)


def sums_kernel(dk, dv, *refs):
    parts, (out_k, out_v) = refs[:-2], refs[-2:]
    rows = dk.shape[0]
    key_sum, value_sum = dk[...], dv[...]
    for part in parts:
        key_sum += part[:rows, :].astype(F32)
        value_sum += part[rows:, :].astype(F32)
    out_k[...] = key_sum.astype(out_k.dtype)
    out_v[...] = value_sum.astype(out_v.dtype)


def add_kernel(first, second, both):
    both[...] = (first[...].astype(F32) + second[...].astype(F32)).astype(BF16)


def token_kernel(x, *refs):
    pass


SMEM = pl.BlockSpec(memory_space=pltpu.SMEM)
VMEM = pl.BlockSpec(memory_space=pltpu.VMEM)
ANY = pl.BlockSpec(memory_space=pl.ANY)


def call(body, outs, in_specs, out_spec=VMEM, scratch=(), aliases=None, flops=0, moved=0):
    return pl.pallas_call(
        body,
        out_shape=[jax.ShapeDtypeStruct(s, t) for s, t in outs],
        in_specs=in_specs,
        out_specs=[out_spec] * len(outs),
        scratch_shapes=list(scratch),
        input_output_aliases=aliases or {},
        compiler_params=pltpu.CompilerParams(vmem_limit_bytes=VMEM_LIMIT),
        cost_estimate=pl.CostEstimate(flops=flops, bytes_accessed=moved, transcendentals=0),
    )


def after(x, *others):
    return call(token_kernel, [(x.shape, x.dtype)], [ANY] * (1 + len(others)), out_spec=ANY, aliases={0: 0})(x, *others)[0]


def partner_of(n, s):
    if n & (n - 1) == 0:
        return lambda i: i ^ s
    return lambda i: lax.rem(i + n - s, n) if not isinstance(i, int) else (i + n - s) % n


def shards(n, queries, keys, values, outputs, out_grads, log_norms, stretch_order):
    rows = queries.shape[0]
    size = rows // 2
    heads = queries.shape[1] // HD
    work = 5 * 2 * rows * rows * heads * HD
    total = 2 * heads * size
    wide = (HD, total)
    tall = (total, HD)
    line = (1, total)
    part_type = ((4 * size, HD), BF16)
    sums_type = ((rows, HD), F32)

    def send(x, pairs):
        return lax.ppermute(x, "ctx", pairs)

    def prepare():
        return call(
            prepare_kernel,
            [(tall, BF16), (tall, BF16), (wide, BF16), (wide, BF16), (line, F32), (line, F32)],
            [VMEM] * 4,
            flops=work,
        )(log_norms, queries, out_grads, outputs)

    def own(same):
        return call(
            own_kernel,
            [(wide, F32), sums_type, sums_type],
            [SMEM] + [VMEM] * 8,
            scratch=[pltpu.VMEM((size, heads * size), BF16)] * 2,
            flops=work,
        )(stretch_order, keys, values, *same)

    def remote(s, kv, same, dqt):
        partner = s if callable(s) else lambda i: i ^ s
        return call(
            functools.partial(remote_kernel, partner),
            [(wide, F32), part_type],
            [SMEM] + [VMEM] * 9,
            scratch=[pltpu.VMEM((size, total), BF16)] * 2,
            aliases={9: 0},
            flops=WEIGHT * work,
        )(stretch_order, *kv, *same, dqt)

    def sums(dk, dv, parts, outs):
        return call(sums_kernel, outs, [VMEM] * (2 + len(parts)))(dk, dv, *parts)

    def add(first, second):
        return call(add_kernel, [part_type], [VMEM] * 2)(first, second)[0]

    last = [(keys.shape, BF16), (values.shape, BF16)]
    if n == 4:
        swap = [[(i, i ^ s) for i in range(n)] for s in range(n)]
        own_rows = (keys, values)
        kv_3 = [send(x, swap[3]) for x in own_rows]
        same = prepare()
        kv_1 = [send(x, swap[1]) for x in own_rows]
        dqt, dk, dv = own(same)
        kv_3 = [after(kv_3[0], same[0]), after(kv_3[1], dk)]
        kv_2 = [send(x, swap[1]) for x in kv_3]
        dqt, part_3 = remote(3, kv_3, same, dqt)
        aside_3 = send(part_3, swap[1])
        kv_1 = [after(x, part_3) for x in kv_1]
        dqt, part_1 = remote(1, kv_1, same, dqt)
        kv_2 = [after(x, part_1) for x in kv_2]
        dqt, part_2 = remote(2, kv_2, same, dqt)
        both = add(after(aside_3, part_2), part_2)
        back_2 = send(both, swap[2])
        back_1 = send(after(part_1, both), swap[1])
        returned = [back_1, back_2]
    else:
        same = prepare()
        dqt, dk, dv = own(same)
        partners = [partner_of(n, s) for s in range(1, n)]
        arrived = [[send(x, [(p(i), i) for i in range(n)]) for x in (keys, values)] for p in partners]
        returned = []
        for p, got in zip(partners, arrived):
            dqt, part = remote(p, got, same, dqt)
            returned.append(send(part, [(i, p(i)) for i in range(n)]))
    (grad_queries,) = call(queries_kernel, [(queries.shape, BF16)], [VMEM], flops=WEIGHT * work)(dqt)
    grad_keys, grad_values = sums(dk, dv, returned, last)
    return grad_queries, grad_keys, grad_values


def solution(mesh):
    return jax.shard_map(
        functools.partial(shards, mesh.shape["ctx"]),
        mesh=mesh,
        in_specs=(
            P(("dp", "ctx"), "tp"),
            P(("dp", "ctx"), "tp"),
            P(("dp", "ctx"), "tp"),
            P(("dp", "ctx"), "tp"),
            P(("dp", "ctx"), "tp"),
            P("tp", ("dp", "ctx")),
            P("dp"),
        ),
        out_specs=(P(("dp", "ctx"), "tp"), P(("dp", "ctx"), "tp"), P(("dp", "ctx"), "tp")),
        check_vma=False,
    )
```

```python
import functools
import math

import jax
import jax.numpy as jnp
from jax import lax
from jax.experimental import pallas as pl
from jax.experimental.pallas import tpu as pltpu
from jax.sharding import PartitionSpec as P

HD = 128
SCALE = HD ** (-0.5)
WEIGHT = 10
LOG2E = math.log2(math.e)
F32 = jnp.float32
BF16 = jnp.bfloat16
VMEM_LIMIT = 48 * 1024 * 1024


def low_terms(start, width, key, value, state, diagonal, ps, ds):
    _, _, qt, gt, norm, delta = state
    size = key.shape[0]
    for at in range(0, width, size):
        cols = pl.ds(start + at, size)
        scores = jnp.dot(key, qt[:, cols], preferred_element_type=F32)
        grad_probs = jnp.dot(value, gt[:, cols], preferred_element_type=F32)
        probs = jnp.exp2(scores * (SCALE * LOG2E) - norm[:, cols])
        if diagonal:
            key_at = lax.broadcasted_iota(jnp.int32, probs.shape, 0)
            query_at = lax.broadcasted_iota(jnp.int32, probs.shape, 1)
            probs = jnp.where(key_at <= query_at, probs, 0.0)
        ps[:, at : at + size] = probs.astype(BF16)
        ds[:, at : at + size] = ((probs * SCALE) * (grad_probs - delta[:, cols])).astype(BF16)


def key_terms(start, width, state, ps, ds):
    q4, g4 = state[:2]
    rows = pl.ds(start, width)
    grad_key = jnp.dot(ds[:, :width], q4[rows, :], preferred_element_type=F32)
    grad_value = jnp.dot(ps[:, :width], g4[rows, :], preferred_element_type=F32)
    return grad_key, grad_value


def prepare_kernel(log_norms, q, g, o, q4, g4, qt, gt, norm, delta):
    size = q.shape[0] // 2
    heads = log_norms.shape[0]
    width = heads * size
    for a in range(2):
        rows = pl.ds(a * size, size)
        for h in range(heads):
            lanes = pl.ds(h * HD, HD)
            cols = pl.ds(a * width + h * size, size)
            query, grad = q[rows, lanes], g[rows, lanes]
            q4[cols, :] = query
            g4[cols, :] = grad
            qt[:, cols] = query.T
            gt[:, cols] = grad.T
            prod = grad.astype(F32) * o[rows, lanes].astype(F32)
            delta[:, cols] = jnp.sum(prod.T, axis=0, keepdims=True)
            norm[:, cols] = log_norms[pl.ds(h, 1), rows] * LOG2E


def own_kernel(order, k, v, q4, g4, qt, gt, norm, delta, dqt, dk, dv, ps, ds):
    me = lax.axis_index("ctx")
    size, width = ps.shape
    state = (q4, g4, qt, gt, norm, delta)
    for a in range(2):
        rows, cols = pl.ds(a * size, size), pl.ds(a * width, width)
        key, value = k[rows, :], v[rows, :]
        low_terms(a * width, width, key, value, state, True, ps, ds)
        dk[rows, :], dv[rows, :] = key_terms(a * width, width, state, ps, ds)
        dqt[:, cols] = jnp.dot(key.T, ds[...], preferred_element_type=F32)
    late = (order[2 * me] < order[2 * me + 1]).astype(jnp.int32)
    start = pl.multiple_of(late * width, width)
    rows = pl.ds(pl.multiple_of((1 - late) * size, size), size)
    key, value = k[rows, :], v[rows, :]
    low_terms(start, width, key, value, state, False, ps, ds)
    grad_key, grad_value = key_terms(start, width, state, ps, ds)
    dk[rows, :] += grad_key
    dv[rows, :] += grad_value
    dqt[:, pl.ds(start, width)] += jnp.dot(key.T, ds[...], preferred_element_type=F32)


def remote_kernel(partner, order, k, v, q4, g4, qt, gt, norm, delta, dqt_in, dqt, part, ps, ds):
    me = lax.axis_index("ctx")
    other = partner(me)
    total = q4.shape[0]
    width = total // 2
    size = ps.shape[0]
    state = (q4, g4, qt, gt, norm, delta)
    for b in range(2):
        rows, values_to = pl.ds(b * size, size), pl.ds((2 + b) * size, size)
        before = dqt_in if b == 0 else dqt
        sees = [order[2 * other + b] < order[2 * me + a] for a in range(2)]
        count = sees[0].astype(jnp.int32) + sees[1].astype(jnp.int32)

        def some(start, span):
            key, value = k[rows, :], v[rows, :]
            low_terms(start, span, key, value, state, False, ps, ds)
            grad_key, grad_value = key_terms(start, span, state, ps, ds)
            part[rows, :] = grad_key.astype(BF16)
            part[values_to, :] = grad_value.astype(BF16)
            cols = pl.ds(start, span)
            dqt[:, cols] = before[:, cols] + jnp.dot(key.T, ds[:, :span], preferred_element_type=F32)

        @pl.when(count == 2)
        def _():
            some(0, total)

        @pl.when(count == 1)
        def _():
            seeing = sees[1].astype(jnp.int32)
            some(pl.multiple_of(seeing * width, width), width)
            if b == 0:
                rest = pl.ds(pl.multiple_of((1 - seeing) * width, width), width)
                dqt[:, rest] = dqt_in[:, rest]

        @pl.when(count == 0)
        def _():
            part[rows, :] = jnp.zeros((size, HD), BF16)
            part[values_to, :] = jnp.zeros((size, HD), BF16)
            if b == 0:
                dqt[...] = dqt_in[...]


def queries_kernel(dqt, dq):
    size = dq.shape[0] // 2
    heads = dq.shape[1] // HD
    for a in range(2):
        for h in range(heads):
            tile = dqt[:, pl.ds((a * heads + h) * size, size)]
            dq[pl.ds(a * size, size), pl.ds(h * HD, HD)] = tile.T.astype(BF16)


def sums_kernel(dk, dv, *refs):
    parts, (out_k, out_v) = refs[:-2], refs[-2:]
    rows = dk.shape[0]
    key_sum, value_sum = dk[...], dv[...]
    for part in parts:
        key_sum += part[:rows, :].astype(F32)
        value_sum += part[rows:, :].astype(F32)
    out_k[...] = key_sum.astype(out_k.dtype)
    out_v[...] = value_sum.astype(out_v.dtype)


def add_kernel(first, second, both):
    both[...] = (first[...].astype(F32) + second[...].astype(F32)).astype(BF16)


def token_kernel(x, *refs):
    pass


SMEM = pl.BlockSpec(memory_space=pltpu.SMEM)
VMEM = pl.BlockSpec(memory_space=pltpu.VMEM)
ANY = pl.BlockSpec(memory_space=pl.ANY)


def call(body, outs, in_specs, out_spec=VMEM, scratch=(), aliases=None, flops=0, moved=0):
    return pl.pallas_call(
        body,
        out_shape=[jax.ShapeDtypeStruct(s, t) for s, t in outs],
        in_specs=in_specs,
        out_specs=[out_spec] * len(outs),
        scratch_shapes=list(scratch),
        input_output_aliases=aliases or {},
        compiler_params=pltpu.CompilerParams(vmem_limit_bytes=VMEM_LIMIT),
        cost_estimate=pl.CostEstimate(flops=flops, bytes_accessed=moved, transcendentals=0),
    )


def after(x, *others):
    return call(token_kernel, [(x.shape, x.dtype)], [ANY] * (1 + len(others)), out_spec=ANY, aliases={0: 0})(x, *others)[0]


def partner_of(n, s):
    if n & (n - 1) == 0:
        return lambda i: i ^ s
    return lambda i: lax.rem(i + n - s, n) if not isinstance(i, int) else (i + n - s) % n


def shards(n, queries, keys, values, outputs, out_grads, log_norms, stretch_order):
    rows = queries.shape[0]
    size = rows // 2
    heads = queries.shape[1] // HD
    work = 5 * 2 * rows * rows * heads * HD
    total = 2 * heads * size
    wide = (HD, total)
    tall = (total, HD)
    line = (1, total)
    part_type = ((4 * size, HD), BF16)
    sums_type = ((rows, HD), F32)

    def send(x, pairs):
        return lax.ppermute(x, "ctx", pairs)

    def prepare():
        return call(
            prepare_kernel,
            [(tall, BF16), (tall, BF16), (wide, BF16), (wide, BF16), (line, F32), (line, F32)],
            [VMEM] * 4,
            flops=work,
        )(log_norms, queries, out_grads, outputs)

    def own(same):
        return call(
            own_kernel,
            [(wide, F32), sums_type, sums_type],
            [SMEM] + [VMEM] * 8,
            scratch=[pltpu.VMEM((size, heads * size), BF16)] * 2,
            flops=work,
        )(stretch_order, keys, values, *same)

    def remote(s, kv, same, dqt):
        partner = s if callable(s) else lambda i: i ^ s
        return call(
            functools.partial(remote_kernel, partner),
            [(wide, F32), part_type],
            [SMEM] + [VMEM] * 9,
            scratch=[pltpu.VMEM((size, total), BF16)] * 2,
            aliases={9: 0},
            flops=WEIGHT * work,
        )(stretch_order, *kv, *same, dqt)

    def sums(dk, dv, parts, outs):
        return call(sums_kernel, outs, [VMEM] * (2 + len(parts)))(dk, dv, *parts)

    def add(first, second):
        return call(add_kernel, [part_type], [VMEM] * 2)(first, second)[0]

    last = [(keys.shape, BF16), (values.shape, BF16)]
    if n == 4:
        swap = [[(i, i ^ s) for i in range(n)] for s in range(n)]
        own_rows = (keys, values)
        kv_3 = [send(x, swap[3]) for x in own_rows]
        same = prepare()
        kv_1 = [send(x, swap[1]) for x in own_rows]
        dqt, dk, dv = own(same)
        kv_3 = [after(x, dk) for x in kv_3]
        kv_2 = [send(x, swap[1]) for x in kv_3]
        dqt, part_3 = remote(3, kv_3, same, dqt)
        aside_3 = send(part_3, swap[1])
        kv_1 = [after(x, part_3) for x in kv_1]
        dqt, part_1 = remote(1, kv_1, same, dqt)
        kv_2 = [after(x, part_1) for x in kv_2]
        dqt, part_2 = remote(2, kv_2, same, dqt)
        both = add(after(aside_3, part_2), part_2)
        back_2 = send(both, swap[2])
        back_1 = send(after(part_1, both), swap[1])
        returned = [back_1, back_2]
    else:
        same = prepare()
        dqt, dk, dv = own(same)
        partners = [partner_of(n, s) for s in range(1, n)]
        arrived = [[send(x, [(p(i), i) for i in range(n)]) for x in (keys, values)] for p in partners]
        returned = []
        for p, got in zip(partners, arrived):
            dqt, part = remote(p, got, same, dqt)
            returned.append(send(part, [(i, p(i)) for i in range(n)]))
    (grad_queries,) = call(queries_kernel, [(queries.shape, BF16)], [VMEM], flops=WEIGHT * work)(dqt)
    grad_keys, grad_values = sums(dk, dv, returned, last)
    return grad_queries, grad_keys, grad_values


def solution(mesh):
    return jax.shard_map(
        functools.partial(shards, mesh.shape["ctx"]),
        mesh=mesh,
        in_specs=(
            P(("dp", "ctx"), "tp"),
            P(("dp", "ctx"), "tp"),
            P(("dp", "ctx"), "tp"),
            P(("dp", "ctx"), "tp"),
            P(("dp", "ctx"), "tp"),
            P("tp", ("dp", "ctx")),
            P("dp"),
        ),
        out_specs=(P(("dp", "ctx"), "tp"), P(("dp", "ctx"), "tp"), P(("dp", "ctx"), "tp")),
        check_vma=False,
    )
```

```python
import functools
import math

import jax
import jax.numpy as jnp
from jax import lax
from jax.experimental import pallas as pl
from jax.experimental.pallas import tpu as pltpu
from jax.sharding import PartitionSpec as P

HD = 128
SCALE = HD ** (-0.5)
WEIGHT = 10
LOG2E = math.log2(math.e)
F32 = jnp.float32
BF16 = jnp.bfloat16
VMEM_LIMIT = 48 * 1024 * 1024


def low_terms(start, width, key, value, state, diagonal, ps, ds):
    _, _, qt, gt, norm, delta = state
    size = key.shape[0]
    for at in range(0, width, size):
        cols = pl.ds(start + at, size)
        scores = jnp.dot(key, qt[:, cols], preferred_element_type=F32)
        grad_probs = jnp.dot(value, gt[:, cols], preferred_element_type=F32)
        probs = jnp.exp2(scores * (SCALE * LOG2E) - norm[:, cols])
        if diagonal:
            key_at = lax.broadcasted_iota(jnp.int32, probs.shape, 0)
            query_at = lax.broadcasted_iota(jnp.int32, probs.shape, 1)
            probs = jnp.where(key_at <= query_at, probs, 0.0)
        ps[:, at : at + size] = probs.astype(BF16)
        ds[:, at : at + size] = ((probs * SCALE) * (grad_probs - delta[:, cols])).astype(BF16)


def key_terms(start, width, state, ps, ds):
    q4, g4 = state[:2]
    rows = pl.ds(start, width)
    grad_key = jnp.dot(ds[:, :width], q4[rows, :], preferred_element_type=F32)
    grad_value = jnp.dot(ps[:, :width], g4[rows, :], preferred_element_type=F32)
    return grad_key, grad_value


def prepare_kernel(log_norms, q, g, o, q4, g4, qt, gt, norm, delta):
    size = q.shape[0] // 2
    heads = log_norms.shape[0]
    width = heads * size
    for a in range(2):
        rows = pl.ds(a * size, size)
        for h in range(heads):
            lanes = pl.ds(h * HD, HD)
            cols = pl.ds(a * width + h * size, size)
            query, grad = q[rows, lanes], g[rows, lanes]
            q4[cols, :] = query
            g4[cols, :] = grad
            qt[:, cols] = query.T
            gt[:, cols] = grad.T
            prod = grad.astype(F32) * o[rows, lanes].astype(F32)
            delta[:, cols] = jnp.sum(prod.T, axis=0, keepdims=True)
            norm[:, cols] = log_norms[pl.ds(h, 1), rows] * LOG2E


def own_kernel(order, k, v, q4, g4, qt, gt, norm, delta, dqt, dk, dv, ps, ds):
    me = lax.axis_index("ctx")
    size, width = ps.shape
    state = (q4, g4, qt, gt, norm, delta)
    for a in range(2):
        rows, cols = pl.ds(a * size, size), pl.ds(a * width, width)
        key, value = k[rows, :], v[rows, :]
        low_terms(a * width, width, key, value, state, True, ps, ds)
        dk[rows, :], dv[rows, :] = key_terms(a * width, width, state, ps, ds)
        dqt[:, cols] = jnp.dot(key.T, ds[...], preferred_element_type=F32)
    late = (order[2 * me] < order[2 * me + 1]).astype(jnp.int32)
    start = pl.multiple_of(late * width, width)
    rows = pl.ds(pl.multiple_of((1 - late) * size, size), size)
    key, value = k[rows, :], v[rows, :]
    low_terms(start, width, key, value, state, False, ps, ds)
    grad_key, grad_value = key_terms(start, width, state, ps, ds)
    dk[rows, :] += grad_key
    dv[rows, :] += grad_value
    dqt[:, pl.ds(start, width)] += jnp.dot(key.T, ds[...], preferred_element_type=F32)


def remote_kernel(partner, order, k, v, q4, g4, qt, gt, norm, delta, dqt_in, dqt, part, ps, ds):
    me = lax.axis_index("ctx")
    other = partner(me)
    total = q4.shape[0]
    width = total // 2
    size = ps.shape[0]
    state = (q4, g4, qt, gt, norm, delta)
    for b in range(2):
        rows, values_to = pl.ds(b * size, size), pl.ds((2 + b) * size, size)
        before = dqt_in if b == 0 else dqt
        sees = [order[2 * other + b] < order[2 * me + a] for a in range(2)]
        count = sees[0].astype(jnp.int32) + sees[1].astype(jnp.int32)

        def some(start, span):
            key, value = k[rows, :], v[rows, :]
            low_terms(start, span, key, value, state, False, ps, ds)
            grad_key, grad_value = key_terms(start, span, state, ps, ds)
            part[rows, :] = grad_key.astype(BF16)
            part[values_to, :] = grad_value.astype(BF16)
            cols = pl.ds(start, span)
            dqt[:, cols] = before[:, cols] + jnp.dot(key.T, ds[:, :span], preferred_element_type=F32)

        @pl.when(count == 2)
        def _():
            some(0, total)

        @pl.when(count == 1)
        def _():
            seeing = sees[1].astype(jnp.int32)
            some(pl.multiple_of(seeing * width, width), width)
            if b == 0:
                rest = pl.ds(pl.multiple_of((1 - seeing) * width, width), width)
                dqt[:, rest] = dqt_in[:, rest]

        @pl.when(count == 0)
        def _():
            part[rows, :] = jnp.zeros((size, HD), BF16)
            part[values_to, :] = jnp.zeros((size, HD), BF16)
            if b == 0:
                dqt[...] = dqt_in[...]


def queries_kernel(dqt, dq):
    size = dq.shape[0] // 2
    heads = dq.shape[1] // HD
    for a in range(2):
        for h in range(heads):
            tile = dqt[:, pl.ds((a * heads + h) * size, size)]
            dq[pl.ds(a * size, size), pl.ds(h * HD, HD)] = tile.T.astype(BF16)


def sums_kernel(dk, dv, *refs):
    parts, (out_k, out_v) = refs[:-2], refs[-2:]
    rows = dk.shape[0]
    key_sum, value_sum = dk[...], dv[...]
    for part in parts:
        key_sum += part[:rows, :].astype(F32)
        value_sum += part[rows:, :].astype(F32)
    out_k[...] = key_sum.astype(out_k.dtype)
    out_v[...] = value_sum.astype(out_v.dtype)


def add_kernel(first, second, both):
    both[...] = (first[...].astype(F32) + second[...].astype(F32)).astype(BF16)


def token_kernel(x, *refs):
    pass


SMEM = pl.BlockSpec(memory_space=pltpu.SMEM)
VMEM = pl.BlockSpec(memory_space=pltpu.VMEM)
ANY = pl.BlockSpec(memory_space=pl.ANY)


def call(body, outs, in_specs, out_spec=VMEM, scratch=(), aliases=None, flops=0, moved=0):
    return pl.pallas_call(
        body,
        out_shape=[jax.ShapeDtypeStruct(s, t) for s, t in outs],
        in_specs=in_specs,
        out_specs=[out_spec] * len(outs),
        scratch_shapes=list(scratch),
        input_output_aliases=aliases or {},
        compiler_params=pltpu.CompilerParams(vmem_limit_bytes=VMEM_LIMIT),
        cost_estimate=pl.CostEstimate(flops=flops, bytes_accessed=moved, transcendentals=0),
    )


def after(x, *others):
    return call(token_kernel, [(x.shape, x.dtype)], [ANY] * (1 + len(others)), out_spec=ANY, aliases={0: 0})(x, *others)[0]


def partner_of(n, s):
    if n & (n - 1) == 0:
        return lambda i: i ^ s
    return lambda i: lax.rem(i + n - s, n) if not isinstance(i, int) else (i + n - s) % n


def shards(n, queries, keys, values, outputs, out_grads, log_norms, stretch_order):
    rows = queries.shape[0]
    size = rows // 2
    heads = queries.shape[1] // HD
    work = 5 * 2 * rows * rows * heads * HD
    total = 2 * heads * size
    wide = (HD, total)
    tall = (total, HD)
    line = (1, total)
    part_type = ((4 * size, HD), BF16)
    sums_type = ((rows, HD), F32)

    def send(x, pairs):
        return lax.ppermute(x, "ctx", pairs)

    def prepare():
        return call(
            prepare_kernel,
            [(tall, BF16), (tall, BF16), (wide, BF16), (wide, BF16), (line, F32), (line, F32)],
            [VMEM] * 4,
            flops=work,
        )(log_norms, queries, out_grads, outputs)

    def own(same):
        return call(
            own_kernel,
            [(wide, F32), sums_type, sums_type],
            [SMEM] + [VMEM] * 8,
            scratch=[pltpu.VMEM((size, heads * size), BF16)] * 2,
            flops=work,
        )(stretch_order, keys, values, *same)

    def remote(s, kv, same, dqt):
        partner = s if callable(s) else lambda i: i ^ s
        return call(
            functools.partial(remote_kernel, partner),
            [(wide, F32), part_type],
            [SMEM] + [VMEM] * 9,
            scratch=[pltpu.VMEM((size, total), BF16)] * 2,
            aliases={9: 0},
            flops=WEIGHT * work,
        )(stretch_order, *kv, *same, dqt)

    def sums(dk, dv, parts, outs):
        return call(sums_kernel, outs, [VMEM] * (2 + len(parts)))(dk, dv, *parts)

    def add(first, second):
        return call(add_kernel, [part_type], [VMEM] * 2)(first, second)[0]

    last = [(keys.shape, BF16), (values.shape, BF16)]
    if n == 4:
        swap = [[(i, i ^ s) for i in range(n)] for s in range(n)]
        own_rows = (keys, values)
        kv_3 = [send(x, swap[3]) for x in own_rows]
        same = prepare()
        kv_1 = [send(x, swap[1]) for x in own_rows]
        dqt, dk, dv = own(same)
        kv_3 = [after(kv_3[0], same[0]), after(kv_3[1], dk)]
        kv_2 = [send(x, swap[1]) for x in kv_3]
        dqt, part_3 = remote(3, kv_3, same, dqt)
        aside_3 = send(part_3, swap[1])
        kv_1 = [after(x, part_3) for x in kv_1]
        dqt, part_1 = remote(1, kv_1, same, dqt)
        kv_2 = [after(x, part_1) for x in kv_2]
        dqt, part_2 = remote(2, kv_2, same, dqt)
        both = add(after(aside_3, part_2), part_2)
        back_2 = send(both, swap[2])
        back_1 = send(after(part_1, both), swap[1])
        dk, dv = sums(dk, dv, [back_1], [sums_type] * 2)
        returned = [back_2]
    else:
        same = prepare()
        dqt, dk, dv = own(same)
        partners = [partner_of(n, s) for s in range(1, n)]
        arrived = [[send(x, [(p(i), i) for i in range(n)]) for x in (keys, values)] for p in partners]
        returned = []
        for p, got in zip(partners, arrived):
            dqt, part = remote(p, got, same, dqt)
            returned.append(send(part, [(i, p(i)) for i in range(n)]))
    (grad_queries,) = call(queries_kernel, [(queries.shape, BF16)], [VMEM], flops=WEIGHT * work)(dqt)
    grad_keys, grad_values = sums(dk, dv, returned, last)
    return grad_queries, grad_keys, grad_values


def solution(mesh):
    return jax.shard_map(
        functools.partial(shards, mesh.shape["ctx"]),
        mesh=mesh,
        in_specs=(
            P(("dp", "ctx"), "tp"),
            P(("dp", "ctx"), "tp"),
            P(("dp", "ctx"), "tp"),
            P(("dp", "ctx"), "tp"),
            P(("dp", "ctx"), "tp"),
            P("tp", ("dp", "ctx")),
            P("dp"),
        ),
        out_specs=(P(("dp", "ctx"), "tp"), P(("dp", "ctx"), "tp"), P(("dp", "ctx"), "tp")),
        check_vma=False,
    )
```
